32 devices in a mesh: group: 4 (over z), member: 8 (over y, x, core).
Axes of the slice: x: 2, y: 2, z: 4, core: 2. Of those that a mesh axis runs over, the one named last changes fastest.
Arguments:
- tokens: bfloat16 [2048, 7168], P('group', 'member'), may hold values from -6 to 6
- grad_output: bfloat16 [2048, 7168], P('group', 'member'), may hold values from -6 to 6
- gate_prob: bfloat16 [2048, 4], P('group'), may hold values from 0.099609375 to 1
- w_gate: bfloat16 [4, 7168, 1024], P('group', 'member'), may hold values from -0.0625 to 0.0625
- w_up: bfloat16 [4, 7168, 1024], P('group', 'member'), may hold values from -0.0625 to 0.0625
- w_down: bfloat16 [4, 1024, 7168], P('group', None, 'member'), may hold values from -0.1875 to 0.1875
- expert_slot: int32 [4], replicated, may hold values from 0 to 3, each once
- block_counts: int32 [4, 4], replicated, may hold values from 0 to 10, as said below
- block_lists: int32 [4, 4, 10], P('group'), may hold values from 0 to 15, as said below
Outputs:
- layer_output: bfloat16 [2048, 7168], P('group', 'member')
- grad_input: bfloat16 [2048, 7168], P('group', 'member')
- grad_w_gate: bfloat16 [4, 7168, 1024], P('group', 'member')
- grad_w_up: bfloat16 [4, 7168, 1024], P('group', 'member')
- grad_w_down: bfloat16 [4, 1024, 7168], P('group', None, 'member')
The draws below stay inside these ranges and needn't reach their ends.
Inputs may be any that keep to these rules, and one draw needn't show every extreme that they name: `block_counts`: each group sends blocks to 1 to 2 experts and some group to exactly 2; each expert receives blocks from 1 to 2 groups and some expert from exactly 2; some count equals 10. `block_lists`: the first block_counts[g, e] entries of a list are distinct blocks of group g; later entries are block numbers that play no part. `expert_slot`: a permutation of the slots; slot s lies on group s.
All inputs are finite; a program needn't handle non-finite values.
Results may differ from the reference program's by a relative error of at most 0.034.
Values may be sent and summed in bfloat16 or wider, within the bound.
A program may use at most 128 MiB of HBM per device.

```python
import math
import jax
import jax.numpy as jnp
from jax import lax

D = 7168
F = 1024
MAXE = 2
MAXB = 10
BLK = 32
NBLK = 16
EXPERTS = 4
TOKENS = 2048
N_GROUP = 4
N_MEMBER = 8


def routing_draw(key):
    first, second, third, fourth, fifth = jax.random.split(jax.random.fold_in(key, 7), 5)
    order = jax.random.permutation(first, EXPERTS)
    cycle = jax.random.permutation(fifth, N_GROUP).astype(jnp.int32)
    position = jnp.zeros((N_GROUP,), jnp.int32).at[cycle].set(jnp.arange(N_GROUP, dtype=jnp.int32))
    layer = jnp.arange(MAXE, dtype=jnp.int32)[:, None]
    group_ids = jnp.arange(N_GROUP, dtype=jnp.int32)[None, :]
    active = jax.random.randint(second, (MAXE, N_GROUP), 0, 2)
    forced = (layer == 0) | (group_ids == cycle[0])
    active = jnp.where(forced, 1, active)
    amounts = jax.random.randint(third, (MAXE, N_GROUP), 1, MAXB + 1)
    amounts = jnp.where((layer == 0) & (group_ids == 0), MAXB, amounts)
    partner = cycle[(position[None, :] + layer) % N_GROUP]
    chosen = order[partner]
    matched = (chosen[:, :, None] == jnp.arange(EXPERTS)[None, None, :]).astype(jnp.int32)
    counts = jnp.sum(matched * (active * amounts)[:, :, None], axis=0)
    keys = jax.random.split(fourth, N_GROUP * EXPERTS)
    lists = jax.vmap(lambda single: jax.random.permutation(single, NBLK)[:MAXB])(keys)
    return (counts.astype(jnp.int32), lists.reshape(N_GROUP, EXPERTS, MAXB).astype(jnp.int32))


def draw_block_counts(key, part):
    return routing_draw(key)[0]


def draw_block_lists(key, part):
    return routing_draw(key)[1]


def levels(rng, dims, shards, low, top_value):
    gain, own = 1.0, jax.random.fold_in(rng, 6)
    for dim, parts in shards:
        draws = jnp.exp(jax.random.uniform(jax.random.fold_in(own, dim), (parts,), jnp.float32, low / len(shards), top_value / len(shards)))
        gain = gain * jnp.repeat(draws, dims[dim] // parts).reshape([-1 if axis == dim else 1 for axis in range(len(dims))])
    return gain


def gaussian(stream_key, shape, width, reach, cuts=(), kind=jnp.bfloat16):
    drawn = width * jax.random.normal(stream_key, shape, jnp.float32)
    if cuts:
        drawn = drawn * levels(stream_key, shape, cuts, -0.22, 0.18)
    return jnp.clip(drawn, -reach, reach).astype(kind)


def setup_inputs(seed: int = 0) -> dict:
    seeds = jax.random.split(jax.random.key(seed), 10)
    tokens = gaussian(seeds[0], (TOKENS, D), 1.0, 6.0, ((0, 4), (1, 8)))
    grad_output = gaussian(seeds[1], (TOKENS, D), 1.0, 6.0, ((0, 4), (1, 8)))
    gate_prob = jnp.clip(jnp.exp(math.log(1.0) - 2.306499 * jax.random.uniform(seeds[2], (TOKENS, EXPERTS), jnp.float32) ** levels(seeds[2], (TOKENS, EXPERTS), ((0, 4),), -0.2, 0.2)), 0.099609375, 1.0).astype(jnp.bfloat16)
    w_gate = gaussian(seeds[3], (EXPERTS, D, F), D ** -0.5, 0.0625, ((0, 4), (1, 8)))
    w_up = gaussian(seeds[4], (EXPERTS, D, F), D ** -0.5, 0.0625, ((0, 4), (1, 8)))
    w_down = gaussian(seeds[5], (EXPERTS, F, D), F ** -0.5, 0.1875, ((0, 4), (2, 8)))
    expert_slot = jax.random.permutation(seeds[6], EXPERTS).astype(jnp.int32)
    block_counts = draw_block_counts(jax.random.fold_in(seeds[9], 71), 0)
    block_lists = draw_block_lists(jax.random.fold_in(seeds[9], 71), 0)
    return {"tokens": tokens, "grad_output": grad_output, "gate_prob": gate_prob, "w_gate": w_gate, "w_up": w_up, "w_down": w_down, "expert_slot": expert_slot, "block_counts": block_counts, "block_lists": block_lists}


def member_sum(left_operand, right_operand):
    count_value = left_operand.shape[0]
    share_portion = D // N_MEMBER
    part_pieces = jnp.einsum("glb,lbv->lgv", left_operand.astype(jnp.float32).reshape(count_value, N_MEMBER, share_portion), right_operand.astype(jnp.float32).reshape(N_MEMBER, share_portion, right_operand.shape[1]))
    part_pieces = lax.optimization_barrier(part_pieces.astype(jnp.bfloat16))
    return jnp.sum(part_pieces.astype(jnp.float32), axis=0)


def expert_ref(input_rows, rows_dy, rows_p, gate_w, up_w, down_w):
    gate = member_sum(input_rows, gate_w)
    up = member_sum(input_rows, up_w)
    sigma = jax.nn.sigmoid(gate)
    hidden_state = (gate * sigma * up).astype(jnp.bfloat16)
    outcome = (rows_p[:, None] * jnp.dot(hidden_state, down_w, preferred_element_type=jnp.float32)).astype(jnp.bfloat16)
    gradient_rows = (rows_p[:, None] * rows_dy.astype(jnp.float32)).astype(jnp.bfloat16)
    grad_hidden = member_sum(gradient_rows, down_w.T)
    gate_gradient = (grad_hidden * up * sigma * (1.0 + gate * (1.0 - sigma))).astype(jnp.bfloat16)
    up_gradient = (grad_hidden * gate * sigma).astype(jnp.bfloat16)
    rows_dx = (jnp.dot(gate_gradient, gate_w.T, preferred_element_type=jnp.float32) + jnp.dot(up_gradient, up_w.T, preferred_element_type=jnp.float32)).astype(jnp.bfloat16)
    part_gate = jnp.dot(input_rows.T, gate_gradient, preferred_element_type=jnp.float32).astype(jnp.bfloat16)
    part_up = jnp.dot(input_rows.T, up_gradient, preferred_element_type=jnp.float32).astype(jnp.bfloat16)
    part_down = jnp.dot(hidden_state.T, gradient_rows, preferred_element_type=jnp.float32).astype(jnp.bfloat16)
    return outcome, rows_dx, part_gate, part_up, part_down


def reference(tokens, grad_output, gate_prob, w_gate, w_up, w_down, expert_slot, block_counts, block_lists):
    in_use = (block_counts > 0).astype(jnp.int32)
    slot_ids = jnp.arange(EXPERTS, dtype=jnp.int32)
    slot_expert = jnp.sum(slot_ids[None, :] * (expert_slot[None, :] == slot_ids[:, None]).astype(jnp.int32), axis=1).astype(jnp.int32)
    tok_blocks = tokens.reshape(N_GROUP, NBLK, BLK, D)
    grad_blocks = grad_output.reshape(N_GROUP, NBLK, BLK, D)
    prob_blocks = gate_prob.reshape(N_GROUP, NBLK, BLK, EXPERTS)
    group_ids = jnp.arange(N_GROUP, dtype=jnp.int32)
    block_ids = jnp.arange(NBLK, dtype=jnp.int32)
    entry_ids = jnp.arange(MAXB, dtype=jnp.int32)

    def per_slot(carry, slot_id):
        out_total, dx_total = carry
        expert_id = slot_expert[slot_id]
        users = in_use[:, expert_id]
        use_rank = jnp.cumsum(users) - 1
        gate_w = w_gate[slot_id]
        up_w = w_up[slot_id]
        down_w = w_down[slot_id]
        total_gate = jnp.zeros((D, F), jnp.float32)
        total_up = jnp.zeros((D, F), jnp.float32)
        total_down = jnp.zeros((F, D), jnp.float32)
        for user in range(MAXE):
            chosen = users * (use_rank == user).astype(jnp.int32)
            valid = jnp.sum(chosen)
            group_id = jnp.sum(chosen * group_ids).astype(jnp.int32)
            count_value = block_counts[group_id, expert_id] * valid
            listed = block_lists[group_id, expert_id].astype(jnp.int32)
            keep_rows = (entry_ids < count_value).astype(jnp.int32)
            input_rows = (tok_blocks[group_id][listed] * keep_rows[:, None, None].astype(jnp.bfloat16)).reshape(MAXB * BLK, D)
            rows_dy = grad_blocks[group_id][listed].reshape(MAXB * BLK, D)
            rows_p = (prob_blocks[group_id][listed][:, :, expert_id].astype(jnp.float32) * keep_rows[:, None].astype(jnp.float32)).reshape(MAXB * BLK)
            outcome, rows_dx, part_gate, part_up, part_down = expert_ref(input_rows, rows_dy, rows_p, gate_w, up_w, down_w)
            placing = ((listed[:, None] == block_ids[None, :]) & (keep_rows[:, None] > 0)).astype(jnp.float32)
            out_total = out_total.at[group_id].add(jnp.einsum("bk,btd->ktd", placing, outcome.astype(jnp.float32).reshape(MAXB, BLK, D)))
            dx_total = dx_total.at[group_id].add(jnp.einsum("bk,btd->ktd", placing, rows_dx.astype(jnp.float32).reshape(MAXB, BLK, D)))
            total_gate = total_gate + part_gate.astype(jnp.float32)
            total_up = total_up + part_up.astype(jnp.float32)
            total_down = total_down + part_down.astype(jnp.float32)
        return (out_total, dx_total), (total_gate.astype(jnp.bfloat16), total_up.astype(jnp.bfloat16), total_down.astype(jnp.bfloat16))

    start = (jnp.zeros((N_GROUP, NBLK, BLK, D), jnp.float32), jnp.zeros((N_GROUP, NBLK, BLK, D), jnp.float32))
    (out_total, dx_total), (grad_w_gate, grad_w_up, grad_w_down) = lax.scan(per_slot, start, slot_ids)
    layer_output = out_total.reshape(N_GROUP * NBLK * BLK, D).astype(jnp.bfloat16)
    grad_input = dx_total.reshape(N_GROUP * NBLK * BLK, D).astype(jnp.bfloat16)
    return (layer_output, grad_input, grad_w_gate, grad_w_up, grad_w_down)
```

```python
import functools
import itertools

import jax
import jax.numpy as jnp
import numpy as np
from jax import lax
from jax.experimental import pallas as pl
from jax.experimental.pallas import tpu as pltpu
from jax.sharding import PartitionSpec as P

MAXE = 2
BLK = 32
HALVES = 2
VMEM_LIMIT = 56 * 1024 * 1024


@functools.lru_cache(None)
def matchings(n):
    found = [
        m
        for m in itertools.product(range(-1, n), repeat=n)
        if len({s for s in m if s >= 0}) == sum(s >= 0 for s in m)
    ]
    return found, {m: i for i, m in enumerate(found)}


@functools.lru_cache(None)
def moving(n):
    found = [m for m in matchings(n)[0] if all(s != g for g, s in enumerate(m))]
    return found, {m: i for i, m in enumerate(found)}


def line_load(m):
    n = len(m)
    worst = 0
    for cut in range(n - 1):
        worst = max(
            worst,
            sum(s > cut >= g for g, s in enumerate(m)),
            sum(0 <= s <= cut < g for g, s in enumerate(m)),
        )
    return worst


@functools.lru_cache(None)
def tables(n):
    found, place = matchings(n)
    moved, moved_place = moving(n)
    load = [line_load(m) for m in found]
    options = [()] + [c for k in (1, 2) for c in itertools.combinations(range(n), k)]
    split = np.zeros((1 << (n * n), 2), np.int32)
    for rows in itertools.product(options, repeat=n):
        if max(sum(s in r for r in rows) for s in range(n)) > MAXE:
            continue
        code = sum(1 << (g * n + s) for g, r in enumerate(rows) for s in r)
        best = None
        ways = [[(r + (-1, -1))[:2], (r + (-1, -1))[:2][::-1]] for r in rows]
        for way in itertools.product(*ways):
            first = place.get(tuple(w[0] for w in way))
            second = place.get(tuple(w[1] for w in way))
            if first is None or second is None:
                continue
            cost = load[first] + load[second]
            if best is None or cost < best[0]:
                best = (cost, first, second)
        split[code] = best[1:]
    inverse = []
    for m in moved:
        back = [-1] * n
        for g, s in enumerate(m):
            if s >= 0:
                back[s] = g
        inverse.append(moved_place[tuple(back)])
    masked = np.zeros((len(found), 1 << n), np.int32)
    for i, m in enumerate(found):
        for bits in range(1 << n):
            masked[i, bits] = moved_place[
                tuple(s if bits >> g & 1 and s != g else -1 for g, s in enumerate(m))
            ]
    return split, np.array(found, np.int32), masked, np.array(inverse, np.int32)


def permute(indices, selves, values, n):
    found, _ = moving(n)

    def branch(m):
        pairs = [(g, s) for g, s in enumerate(m) if s >= 0]
        if not pairs:
            return lambda v: jnp.zeros_like(v)
        return lambda v: lax.ppermute(v, "group", pairs)

    branches = [branch(m) for m in found]

    def step(_, item):
        index, stays, value = item
        arrived = lax.switch(index, branches, value)
        return None, jnp.where(stays, value, arrived)

    return lax.scan(step, None, (indices, selves, values))[1]


def pick_kernel(list_ref, keep_ref, expert_ref, tok_ref, dy_ref, prob_ref, out_ref):
    chunks, _, rows, width = out_ref.shape
    layers, halves = MAXE, chunks // MAXE
    per_half = rows // BLK
    lanes = lax.broadcasted_iota(jnp.int32, (BLK, prob_ref.shape[1]), 1)
    for layer in range(layers):
        for half in range(halves):

            @pl.loop(0, per_half)
            def _(j):
                entry = half * per_half + j
                keep = keep_ref[layer, entry]
                source = pl.ds(pl.multiple_of(list_ref[layer, entry] * BLK, BLK), BLK)
                target = pl.ds(pl.multiple_of(j * BLK, BLK), BLK)

                @pl.when(keep > 0)
                def _():
                    p = jnp.sum(
                        jnp.where(
                            lanes == expert_ref[layer], prob_ref[source, :].astype(jnp.float32), 0.0
                        ),
                        axis=1,
                        keepdims=True,
                    )
                    out_ref[layer * halves + half, 0, target, :] = tok_ref[source, :]
                    out_ref[layer * halves + half, 1, target, :] = (
                        p * dy_ref[source, :].astype(jnp.float32)
                    ).astype(out_ref.dtype)

                @pl.when(keep == 0)
                def _():
                    nothing = jnp.zeros((BLK, width), out_ref.dtype)
                    out_ref[layer * halves + half, 0, target, :] = nothing
                    out_ref[layer * halves + half, 1, target, :] = nothing


def put_kernel(pos_ref, expert_ref, prob_ref, home_ref, out_ref, dx_ref):
    halves = home_ref.shape[0] // MAXE
    per_half = home_ref.shape[2] // BLK
    width = out_ref.shape[1]
    lanes = lax.broadcasted_iota(jnp.int32, (BLK, prob_ref.shape[1]), 1)

    @pl.loop(0, out_ref.shape[0] // BLK)
    def _(block):
        target = pl.ds(pl.multiple_of(block * BLK, BLK), BLK)
        probs = prob_ref[target, :].astype(jnp.float32)
        out = jnp.zeros((BLK, width), jnp.float32)
        dx = jnp.zeros((BLK, width), jnp.float32)
        for layer in range(MAXE):
            pos = pos_ref[layer, block]
            p = jnp.sum(jnp.where(lanes == expert_ref[layer], probs, 0.0), axis=1, keepdims=True)
            there = jnp.maximum(pos, 0)
            chunk = layer * halves + there // per_half
            source = pl.ds(pl.multiple_of(there % per_half * BLK, BLK), BLK)
            out += jnp.where(pos >= 0, home_ref[chunk, 0, source, :].astype(jnp.float32), 0.0) * p
            dx += jnp.where(pos >= 0, home_ref[chunk, 1, source, :].astype(jnp.float32), 0.0)
        out_ref[target, :] = out.astype(out_ref.dtype)
        dx_ref[target, :] = dx.astype(dx_ref.dtype)


SMEM = pl.BlockSpec(memory_space=pltpu.SMEM)
VMEM = pl.BlockSpec(memory_space=pltpu.VMEM)


def body(
    tokens, grad_output, gate_prob, w_gate, w_up, w_down, expert_slot, block_counts, block_lists
):
    token_total, width = tokens.shape
    hidden_total = w_gate.shape[2]
    n = lax.axis_size("group")
    members = lax.axis_size("member")
    block_total = token_total // BLK
    entry_total = block_lists.shape[2]
    experts = block_counts.shape[1]
    per_half = -(-entry_total // HALVES)
    entry_pad = per_half * HALVES
    half_rows = per_half * BLK
    me = lax.axis_index("group")
    wg, wu, wd = w_gate[0], w_up[0], w_down[0]

    slot_ids = jnp.arange(n, dtype=jnp.int32)
    at_slot = (expert_slot[:, None] == slot_ids[None, :]).astype(jnp.int32)
    counts = jnp.sum(block_counts[:, :, None] * at_slot[None, :, :], axis=1)
    slot_expert = jnp.sum(at_slot * jnp.arange(experts, dtype=jnp.int32)[:, None], axis=0)
    used = counts > 0
    small = n <= 4
    if small:
        split, found, masked, inverse = tables(n)
        bits = (1 << np.arange(n * n)).reshape(n, n).astype(np.int32)
        code = jnp.sum(used * bits)
        whole = jnp.asarray(split)[code]
        dests = jnp.asarray(found)[whole]
        amounts_all = jnp.sum(
            jnp.where(dests[:, :, None] == slot_ids[None, None, :], counts[None, :, :], 0), axis=2
        )
        limits = (jnp.arange(HALVES, dtype=jnp.int32) * per_half)[None, :, None]
        more = amounts_all[:, None, :] > limits
        mask = jnp.sum(more * (1 << slot_ids)[None, None, :], axis=2)
        index = jnp.asarray(masked)[whole[:, None], mask].reshape(MAXE * HALVES)
        my_dest = lax.dynamic_index_in_dim(dests, me, 1, keepdims=False)
    else:
        rank = jnp.cumsum(used.astype(jnp.int32), axis=1) - 1
        mine = lax.dynamic_index_in_dim(used, me, 0, keepdims=False)
        my_rank = lax.dynamic_index_in_dim(rank, me, 0, keepdims=False)
        hit = mine[None, :] & (my_rank[None, :] == jnp.arange(MAXE, dtype=jnp.int32)[:, None])
        my_dest = jnp.sum(hit * (slot_ids + 1)[None, :], axis=1) - 1
    my_counts = lax.dynamic_index_in_dim(counts, me, 0, keepdims=False)
    dest_hit = my_dest[:, None] == slot_ids[None, :]
    my_amount = jnp.sum(jnp.where(dest_hit, my_counts[None, :], 0), axis=1)
    my_expert = jnp.sum(jnp.where(dest_hit, slot_expert[None, :], 0), axis=1).astype(jnp.int32)
    expert_hit = my_expert[:, None] == jnp.arange(experts, dtype=jnp.int32)[None, :]
    listed = jnp.sum(jnp.where(expert_hit[:, :, None], block_lists[0][None], 0), axis=1)
    listed = jnp.pad(listed, ((0, 0), (0, entry_pad - entry_total)))
    entries = jnp.arange(entry_pad, dtype=jnp.int32)
    keep = (entries[None, :] < my_amount[:, None]).astype(jnp.int32)
    blocks = jnp.arange(block_total, dtype=jnp.int32)
    lies = (listed[:, :, None] == blocks[None, None, :]) & (keep[:, :, None] > 0)
    position = jnp.sum(lies * (entries + 1)[None, :, None], axis=1).astype(jnp.int32) - 1

    sent = pl.pallas_call(
        pick_kernel,
        out_shape=jax.ShapeDtypeStruct((MAXE * HALVES, 2, half_rows, width), jnp.bfloat16),
        in_specs=[SMEM, SMEM, SMEM, VMEM, VMEM, VMEM],
        out_specs=VMEM,
        compiler_params=pltpu.CompilerParams(vmem_limit_bytes=VMEM_LIMIT),
    )(listed, keep, my_expert, tokens, grad_output, gate_prob)

    if small:
        stays = jnp.repeat(my_dest == me, HALVES)
        got = permute(index, stays, sent, n)
    else:
        place = (my_dest[:, None] == slot_ids[None, :]).astype(jnp.bfloat16)
        spread = jnp.einsum("ln,lhkrw->nhkrw", place, sent.reshape(MAXE, HALVES, 2, half_rows, width))
        arrived = lax.all_to_all(spread, "group", split_axis=0, concat_axis=0, tiled=True)
        users = lax.dynamic_index_in_dim(used, me, 1, keepdims=False).astype(jnp.int32)
        user_rank = jnp.cumsum(users) - 1
        take = (
            (user_rank[None, :] == jnp.arange(MAXE, dtype=jnp.int32)[:, None]) & (users[None, :] > 0)
        ).astype(jnp.bfloat16)
        taken = jnp.einsum("ln,nhkrw->lhkrw", take, arrived)
        got = taken.reshape(sent.shape)
    rows_x = got[:, 0].reshape(-1, width)
    rows_dy = got[:, 1].reshape(-1, width)
    f32 = jnp.float32

    def dot(a, b, dims):
        return lax.dot_general(a, b, (dims, ((), ())), preferred_element_type=f32).astype(
            jnp.bfloat16
        )

    part_gate = dot(rows_x, wg, ((1,), (0,)))
    part_up = dot(rows_x, wu, ((1,), (0,)))
    part_back = dot(rows_dy, wd, ((1,), (1,)))
    parts = jnp.concatenate([part_gate, part_up, part_back], axis=1)
    summed = lax.psum_scatter(parts, "member", scatter_dimension=0, tiled=True)
    gate, up, back = jnp.split(summed.astype(f32), 3, axis=1)
    s = jax.nn.sigmoid(gate)
    acts = jnp.concatenate(
        [
            (gate * s * up).astype(jnp.bfloat16),
            (back * up * s * (1.0 + gate * (1.0 - s))).astype(jnp.bfloat16),
            (back * gate * s).astype(jnp.bfloat16),
        ],
        axis=1,
    )
    acts = lax.all_gather(acts, "member", axis=0, tiled=True)
    hidden, d_gate, d_up = jnp.split(acts, 3, axis=1)
    out = dot(hidden, wd, ((1,), (0,)))
    dx = (
        lax.dot_general(d_gate, wg, (((1,), (1,)), ((), ())), preferred_element_type=f32)
        + lax.dot_general(d_up, wu, (((1,), (1,)), ((), ())), preferred_element_type=f32)
    ).astype(jnp.bfloat16)
    chunk = (MAXE * HALVES, half_rows, width)
    both = jnp.stack([out.reshape(chunk), dx.reshape(chunk)], axis=1)
    if small:
        own_dests = jnp.sum(jnp.where(dests == me, slot_ids[None, :] + 1, 0), axis=1) - 1
        home = permute(jnp.asarray(inverse)[index], jnp.repeat(own_dests == me, HALVES), both, n)
    else:
        spread = jnp.einsum("ln,lhkrw->nhkrw", take, both.reshape(MAXE, HALVES, 2, half_rows, width))
        arrived = lax.all_to_all(spread, "group", split_axis=0, concat_axis=0, tiled=True)
        taken = jnp.einsum("ln,nhkrw->lhkrw", place, arrived)
        home = taken.reshape(both.shape)
    grad_gate = dot(rows_x, d_gate, ((0,), (0,)))
    grad_up = dot(rows_x, d_up, ((0,), (0,)))
    grad_down = dot(hidden, rows_dy, ((0,), (0,)))
    layer_output, grad_input = pl.pallas_call(
        put_kernel,
        out_shape=[jax.ShapeDtypeStruct(tokens.shape, jnp.bfloat16)] * 2,
        in_specs=[SMEM, SMEM, VMEM] + [VMEM],
        out_specs=[VMEM, VMEM],
        compiler_params=pltpu.CompilerParams(vmem_limit_bytes=VMEM_LIMIT),
    )(position, my_expert, gate_prob, home)
    return (layer_output, grad_input, grad_gate[None], grad_up[None], grad_down[None])


def solution(mesh):
    in_specs = (
        P("group", "member"),
        P("group", "member"),
        P("group", None),
        P("group", "member", None),
        P("group", "member", None),
        P("group", None, "member"),
        P(),
        P(),
        P("group", None, None),
    )
    out_specs = (
        P("group", "member"),
        P("group", "member"),
        P("group", "member", None),
        P("group", "member", None),
        P("group", None, "member"),
    )
    return jax.shard_map(body, mesh=mesh, in_specs=in_specs, out_specs=out_specs, check_vma=False)
```

```python
import functools
import itertools

import jax
import jax.numpy as jnp
import numpy as np
from jax import lax
from jax.experimental import pallas as pl
from jax.experimental.pallas import tpu as pltpu
from jax.sharding import PartitionSpec as P

MAXE = 2
BLK = 32
HALVES = 1
VMEM_LIMIT = 56 * 1024 * 1024


@functools.lru_cache(None)
def matchings(n):
    found = [
        m
        for m in itertools.product(range(-1, n), repeat=n)
        if len({s for s in m if s >= 0}) == sum(s >= 0 for s in m)
    ]
    return found, {m: i for i, m in enumerate(found)}


@functools.lru_cache(None)
def moving(n):
    found = [m for m in matchings(n)[0] if all(s != g for g, s in enumerate(m))]
    return found, {m: i for i, m in enumerate(found)}


def line_load(m):
    n = len(m)
    worst = 0
    for cut in range(n - 1):
        worst = max(
            worst,
            sum(s > cut >= g for g, s in enumerate(m)),
            sum(0 <= s <= cut < g for g, s in enumerate(m)),
        )
    return worst


@functools.lru_cache(None)
def tables(n):
    found, place = matchings(n)
    moved, moved_place = moving(n)
    load = [line_load(m) for m in found]
    options = [()] + [c for k in (1, 2) for c in itertools.combinations(range(n), k)]
    split = np.zeros((1 << (n * n), 2), np.int32)
    for rows in itertools.product(options, repeat=n):
        if max(sum(s in r for r in rows) for s in range(n)) > MAXE:
            continue
        code = sum(1 << (g * n + s) for g, r in enumerate(rows) for s in r)
        best = None
        ways = [[(r + (-1, -1))[:2], (r + (-1, -1))[:2][::-1]] for r in rows]
        for way in itertools.product(*ways):
            first = place.get(tuple(w[0] for w in way))
            second = place.get(tuple(w[1] for w in way))
            if first is None or second is None:
                continue
            cost = load[first] + load[second]
            if best is None or cost < best[0]:
                best = (cost, first, second)
        split[code] = best[1:]
    inverse = []
    for m in moved:
        back = [-1] * n
        for g, s in enumerate(m):
            if s >= 0:
                back[s] = g
        inverse.append(moved_place[tuple(back)])
    masked = np.zeros((len(found), 1 << n), np.int32)
    for i, m in enumerate(found):
        for bits in range(1 << n):
            masked[i, bits] = moved_place[
                tuple(s if bits >> g & 1 and s != g else -1 for g, s in enumerate(m))
            ]
    return split, np.array(found, np.int32), masked, np.array(inverse, np.int32)


def permute(indices, selves, values, n):
    found, _ = moving(n)

    def branch(m):
        pairs = [(g, s) for g, s in enumerate(m) if s >= 0]
        if not pairs:
            return lambda v: jnp.zeros_like(v)
        return lambda v: lax.ppermute(v, "group", pairs)

    branches = [branch(m) for m in found]

    def step(_, item):
        index, stays, value = item
        arrived = lax.switch(index, branches, value)
        return None, jnp.where(stays, value, arrived)

    return lax.scan(step, None, (indices, selves, values))[1]


def pick_kernel(list_ref, keep_ref, expert_ref, tok_ref, dy_ref, prob_ref, out_ref):
    chunks, _, rows, width = out_ref.shape
    layers, halves = MAXE, chunks // MAXE
    per_half = rows // BLK
    lanes = lax.broadcasted_iota(jnp.int32, (BLK, prob_ref.shape[1]), 1)
    for layer in range(layers):
        for half in range(halves):

            @pl.loop(0, per_half)
            def _(j):
                entry = half * per_half + j
                keep = keep_ref[layer, entry]
                source = pl.ds(pl.multiple_of(list_ref[layer, entry] * BLK, BLK), BLK)
                target = pl.ds(pl.multiple_of(j * BLK, BLK), BLK)

                @pl.when(keep > 0)
                def _():
                    p = jnp.sum(
                        jnp.where(
                            lanes == expert_ref[layer], prob_ref[source, :].astype(jnp.float32), 0.0
                        ),
                        axis=1,
                        keepdims=True,
                    )
                    out_ref[layer * halves + half, 0, target, :] = tok_ref[source, :]
                    out_ref[layer * halves + half, 1, target, :] = (
                        p * dy_ref[source, :].astype(jnp.float32)
                    ).astype(out_ref.dtype)

                @pl.when(keep == 0)
                def _():
                    nothing = jnp.zeros((BLK, width), out_ref.dtype)
                    out_ref[layer * halves + half, 0, target, :] = nothing
                    out_ref[layer * halves + half, 1, target, :] = nothing


def put_kernel(pos_ref, expert_ref, prob_ref, home_ref, out_ref, dx_ref):
    halves = home_ref.shape[0] // MAXE
    per_half = home_ref.shape[2] // BLK
    width = out_ref.shape[1]
    lanes = lax.broadcasted_iota(jnp.int32, (BLK, prob_ref.shape[1]), 1)

    @pl.loop(0, out_ref.shape[0] // BLK)
    def _(block):
        target = pl.ds(pl.multiple_of(block * BLK, BLK), BLK)
        probs = prob_ref[target, :].astype(jnp.float32)
        out = jnp.zeros((BLK, width), jnp.float32)
        dx = jnp.zeros((BLK, width), jnp.float32)
        for layer in range(MAXE):
            pos = pos_ref[layer, block]
            p = jnp.sum(jnp.where(lanes == expert_ref[layer], probs, 0.0), axis=1, keepdims=True)
            there = jnp.maximum(pos, 0)
            chunk = layer * halves + there // per_half
            source = pl.ds(pl.multiple_of(there % per_half * BLK, BLK), BLK)
            out += jnp.where(pos >= 0, home_ref[chunk, 0, source, :].astype(jnp.float32), 0.0) * p
            dx += jnp.where(pos >= 0, home_ref[chunk, 1, source, :].astype(jnp.float32), 0.0)
        out_ref[target, :] = out.astype(out_ref.dtype)
        dx_ref[target, :] = dx.astype(dx_ref.dtype)


MESH = pl.DeviceIdType.MESH
TILE = 16


def member_kernel(
    gate_ref, up_ref, back_ref, hid_ref, dg_ref, du_ref,
    recv0, recv1, recv2, send1, send2, kept, send_sem, recv_sem,
):
    ins, outs = (gate_ref, up_ref, back_ref), (hid_ref, dg_ref, du_ref)
    total, width = gate_ref.shape
    half, quarter, eighth, lanes = total // 2, total // 4, total // 8, width // 2
    f32 = jnp.float32
    m = lax.axis_index("member")
    core, x, y = m % 2, (m // 2) % 2, m // 4
    other, beside, across = m + 1 - 2 * core, m + 2 - 4 * x, m + 4 - 8 * y

    barrier = pltpu.get_barrier_semaphore()
    for partner in (other, beside, across):
        pl.semaphore_signal(barrier, inc=1, device_id={"member": partner}, device_id_type=MESH)
    pl.semaphore_wait(barrier, 3)

    first = ((x, beside), (y, across))
    second = ((y, across), (x, beside))
    columns = [pl.ds(h * lanes, lanes) for h in range(2)]
    copies = {}

    def rows(start, count):
        return pl.ds(pl.multiple_of(start, TILE), count)

    def send(step, h, k, source, target, to):
        copies[step, h, k] = pltpu.make_async_remote_copy(
            src_ref=source,
            dst_ref=target,
            send_sem=send_sem.at[step, h, k],
            recv_sem=recv_sem.at[step, h, k],
            device_id={"member": to},
            device_id_type=MESH,
        )
        copies[step, h, k].start()

    def arrived(step, h):
        for k in range(3):
            copies[step, h, k].wait_recv()

    for h in range(2):
        for k in range(3):
            source = ins[k].at[rows((1 - core) * half, half), columns[h]]
            send(0, h, k, source, recv0.at[h, k], other)
    for h in range(2):
        bit, to = first[h]
        arrived(0, h)

        def pair(start, k):
            mine = ins[k][rows(core * half + start, TILE), columns[h]].astype(f32)
            return mine + recv0[h, k, rows(start, TILE), :].astype(f32)

        @pl.loop(0, quarter // TILE)
        def _(t):
            for k in range(3):
                value = pair((1 - bit) * quarter + t * TILE, k)
                send1[h, k, rows(t * TILE, TILE), :] = value.astype(jnp.bfloat16)

        for k in range(3):
            send(1, h, k, send1.at[h, k], recv1.at[h, k], to)

        @pl.loop(0, quarter // TILE)
        def _(t):
            for k in range(3):
                kept[h, k, rows(t * TILE, TILE), :] = pair(bit * quarter + t * TILE, k)

    for h in range(2):
        bit, to = second[h]
        arrived(1, h)

        @pl.loop(0, eighth // TILE)
        def _(t):
            for k in range(3):
                at = rows((1 - bit) * eighth + t * TILE, TILE)
                value = kept[h, k, at, :] + recv1[h, k, at, :].astype(f32)
                send2[h, k, rows(t * TILE, TILE), :] = value.astype(jnp.bfloat16)

        for k in range(3):
            send(2, h, k, send2.at[h, k], recv2.at[h, k], to)

    for h in range(2):
        bit, to = second[h]
        arrived(2, h)
        home = core * half + first[h][0] * quarter + bit * eighth

        @pl.loop(0, eighth // TILE)
        def _(t):
            at = rows(bit * eighth + t * TILE, TILE)
            gate, up, back = (
                kept[h, k, at, :]
                + recv1[h, k, at, :].astype(f32)
                + recv2[h, k, rows(t * TILE, TILE), :].astype(f32)
                for k in range(3)
            )
            there = rows(home + t * TILE, TILE)
            for ref, value in zip(outs, activations(gate, up, back)):
                ref[there, columns[h]] = value

        for k in range(3):
            block = outs[k].at[rows(home, eighth), columns[h]]
            send(3, h, k, block, block, to)
    for h in range(2):
        bit, to = first[h]
        arrived(3, h)
        for k in range(3):
            block = outs[k].at[rows(core * half + bit * quarter, quarter), columns[h]]
            send(4, h, k, block, block, to)
    for h in range(2):
        arrived(4, h)
        for k in range(3):
            block = outs[k].at[rows(core * half, half), columns[h]]
            send(5, h, k, block, block, other)
    for h in range(2):
        arrived(5, h)
    for copy in copies.values():
        copy.wait_send()


def member_call(gate, up, back):
    total, width = gate.shape
    lanes = width // 2
    bf16 = jnp.bfloat16
    return pl.pallas_call(
        member_kernel,
        out_shape=[jax.ShapeDtypeStruct(gate.shape, bf16)] * 3,
        in_specs=[VMEM] * 3,
        out_specs=[VMEM] * 3,
        scratch_shapes=[
            pltpu.VMEM((2, 3, total // 2, lanes), bf16),
            pltpu.VMEM((2, 3, total // 4, lanes), bf16),
            pltpu.VMEM((2, 3, total // 8, lanes), bf16),
            pltpu.VMEM((2, 3, total // 4, lanes), bf16),
            pltpu.VMEM((2, 3, total // 8, lanes), bf16),
            pltpu.VMEM((2, 3, total // 4, lanes), jnp.float32),
            pltpu.SemaphoreType.DMA((6, 2, 3)),
            pltpu.SemaphoreType.DMA((6, 2, 3)),
        ],
        compiler_params=pltpu.CompilerParams(
            collective_id=0, has_side_effects=True, vmem_limit_bytes=VMEM_LIMIT
        ),
    )(gate, up, back)


def activations(gate, up, back):
    s = jax.nn.sigmoid(gate)
    return (
        (gate * s * up).astype(jnp.bfloat16),
        (back * up * s * (1.0 + gate * (1.0 - s))).astype(jnp.bfloat16),
        (back * gate * s).astype(jnp.bfloat16),
    )


SMEM = pl.BlockSpec(memory_space=pltpu.SMEM)
VMEM = pl.BlockSpec(memory_space=pltpu.VMEM)


def body(
    tokens, grad_output, gate_prob, w_gate, w_up, w_down, expert_slot, block_counts, block_lists
):
    token_total, width = tokens.shape
    hidden_total = w_gate.shape[2]
    n = lax.axis_size("group")
    members = lax.axis_size("member")
    block_total = token_total // BLK
    entry_total = block_lists.shape[2]
    experts = block_counts.shape[1]
    per_half = -(-entry_total // HALVES)
    entry_pad = per_half * HALVES
    half_rows = per_half * BLK
    me = lax.axis_index("group")
    wg, wu, wd = w_gate[0], w_up[0], w_down[0]

    slot_ids = jnp.arange(n, dtype=jnp.int32)
    at_slot = (expert_slot[:, None] == slot_ids[None, :]).astype(jnp.int32)
    counts = jnp.sum(block_counts[:, :, None] * at_slot[None, :, :], axis=1)
    slot_expert = jnp.sum(at_slot * jnp.arange(experts, dtype=jnp.int32)[:, None], axis=0)
    used = counts > 0
    small = n <= 4
    if small:
        split, found, masked, inverse = tables(n)
        bits = (1 << np.arange(n * n)).reshape(n, n).astype(np.int32)
        code = jnp.sum(used * bits)
        whole = jnp.asarray(split)[code]
        dests = jnp.asarray(found)[whole]
        amounts_all = jnp.sum(
            jnp.where(dests[:, :, None] == slot_ids[None, None, :], counts[None, :, :], 0), axis=2
        )
        limits = (jnp.arange(HALVES, dtype=jnp.int32) * per_half)[None, :, None]
        more = amounts_all[:, None, :] > limits
        mask = jnp.sum(more * (1 << slot_ids)[None, None, :], axis=2)
        index = jnp.asarray(masked)[whole[:, None], mask].reshape(MAXE * HALVES)
        my_dest = lax.dynamic_index_in_dim(dests, me, 1, keepdims=False)
    else:
        rank = jnp.cumsum(used.astype(jnp.int32), axis=1) - 1
        mine = lax.dynamic_index_in_dim(used, me, 0, keepdims=False)
        my_rank = lax.dynamic_index_in_dim(rank, me, 0, keepdims=False)
        hit = mine[None, :] & (my_rank[None, :] == jnp.arange(MAXE, dtype=jnp.int32)[:, None])
        my_dest = jnp.sum(hit * (slot_ids + 1)[None, :], axis=1) - 1
    my_counts = lax.dynamic_index_in_dim(counts, me, 0, keepdims=False)
    dest_hit = my_dest[:, None] == slot_ids[None, :]
    my_amount = jnp.sum(jnp.where(dest_hit, my_counts[None, :], 0), axis=1)
    my_expert = jnp.sum(jnp.where(dest_hit, slot_expert[None, :], 0), axis=1).astype(jnp.int32)
    expert_hit = my_expert[:, None] == jnp.arange(experts, dtype=jnp.int32)[None, :]
    listed = jnp.sum(jnp.where(expert_hit[:, :, None], block_lists[0][None], 0), axis=1)
    listed = jnp.pad(listed, ((0, 0), (0, entry_pad - entry_total)))
    entries = jnp.arange(entry_pad, dtype=jnp.int32)
    keep = (entries[None, :] < my_amount[:, None]).astype(jnp.int32)
    blocks = jnp.arange(block_total, dtype=jnp.int32)
    lies = (listed[:, :, None] == blocks[None, None, :]) & (keep[:, :, None] > 0)
    position = jnp.sum(lies * (entries + 1)[None, :, None], axis=1).astype(jnp.int32) - 1

    sent = pl.pallas_call(
        pick_kernel,
        out_shape=jax.ShapeDtypeStruct((MAXE * HALVES, 2, half_rows, width), jnp.bfloat16),
        in_specs=[SMEM, SMEM, SMEM, VMEM, VMEM, VMEM],
        out_specs=VMEM,
        compiler_params=pltpu.CompilerParams(vmem_limit_bytes=VMEM_LIMIT),
    )(listed, keep, my_expert, tokens, grad_output, gate_prob)

    if small:
        stays = jnp.repeat(my_dest == me, HALVES)
        got = permute(index, stays, sent, n)
    else:
        place = (my_dest[:, None] == slot_ids[None, :]).astype(jnp.bfloat16)
        spread = jnp.einsum("ln,lhkrw->nhkrw", place, sent.reshape(MAXE, HALVES, 2, half_rows, width))
        arrived = lax.all_to_all(spread, "group", split_axis=0, concat_axis=0, tiled=True)
        users = lax.dynamic_index_in_dim(used, me, 1, keepdims=False).astype(jnp.int32)
        user_rank = jnp.cumsum(users) - 1
        take = (
            (user_rank[None, :] == jnp.arange(MAXE, dtype=jnp.int32)[:, None]) & (users[None, :] > 0)
        ).astype(jnp.bfloat16)
        taken = jnp.einsum("ln,nhkrw->lhkrw", take, arrived)
        got = taken.reshape(sent.shape)
    rows_x = got[:, 0].reshape(-1, width)
    rows_dy = got[:, 1].reshape(-1, width)
    f32 = jnp.float32

    def dot(a, b, dims):
        return lax.dot_general(a, b, (dims, ((), ())), preferred_element_type=f32).astype(
            jnp.bfloat16
        )

    part_gate = dot(rows_x, wg, ((1,), (0,)))
    part_up = dot(rows_x, wu, ((1,), (0,)))
    part_back = dot(rows_dy, wd, ((1,), (1,)))
    if members == 8 and rows_x.shape[0] % (8 * TILE) == 0:
        hidden, d_gate, d_up = member_call(part_gate, part_up, part_back)
    else:
        parts = jnp.concatenate([part_gate, part_up, part_back], axis=1)
        summed = lax.psum_scatter(parts, "member", scatter_dimension=0, tiled=True)
        acts = jnp.concatenate(activations(*jnp.split(summed.astype(f32), 3, axis=1)), axis=1)
        acts = lax.all_gather(acts, "member", axis=0, tiled=True)
        hidden, d_gate, d_up = jnp.split(acts, 3, axis=1)
    out = dot(hidden, wd, ((1,), (0,)))
    dx = (
        lax.dot_general(d_gate, wg, (((1,), (1,)), ((), ())), preferred_element_type=f32)
        + lax.dot_general(d_up, wu, (((1,), (1,)), ((), ())), preferred_element_type=f32)
    ).astype(jnp.bfloat16)
    chunk = (MAXE * HALVES, half_rows, width)
    both = jnp.stack([out.reshape(chunk), dx.reshape(chunk)], axis=1)
    if small:
        own_dests = jnp.sum(jnp.where(dests == me, slot_ids[None, :] + 1, 0), axis=1) - 1
        home = permute(jnp.asarray(inverse)[index], jnp.repeat(own_dests == me, HALVES), both, n)
    else:
        spread = jnp.einsum("ln,lhkrw->nhkrw", take, both.reshape(MAXE, HALVES, 2, half_rows, width))
        arrived = lax.all_to_all(spread, "group", split_axis=0, concat_axis=0, tiled=True)
        taken = jnp.einsum("ln,nhkrw->lhkrw", place, arrived)
        home = taken.reshape(both.shape)
    grad_gate = dot(rows_x, d_gate, ((0,), (0,)))
    grad_up = dot(rows_x, d_up, ((0,), (0,)))
    grad_down = dot(hidden, rows_dy, ((0,), (0,)))
    layer_output, grad_input = pl.pallas_call(
        put_kernel,
        out_shape=[jax.ShapeDtypeStruct(tokens.shape, jnp.bfloat16)] * 2,
        in_specs=[SMEM, SMEM, VMEM] + [VMEM],
        out_specs=[VMEM, VMEM],
        compiler_params=pltpu.CompilerParams(vmem_limit_bytes=VMEM_LIMIT),
    )(position, my_expert, gate_prob, home)
    return (layer_output, grad_input, grad_gate[None], grad_up[None], grad_down[None])


def solution(mesh):
    in_specs = (
        P("group", "member"),
        P("group", "member"),
        P("group", None),
        P("group", "member", None),
        P("group", "member", None),
        P("group", None, "member"),
        P(),
        P(),
        P("group", None, None),
    )
    out_specs = (
        P("group", "member"),
        P("group", "member"),
        P("group", "member", None),
        P("group", "member", None),
        P("group", None, "member"),
    )
    return jax.shard_map(body, mesh=mesh, in_specs=in_specs, out_specs=out_specs, check_vma=False)
```

```python
import functools
import itertools

import jax
import jax.numpy as jnp
import numpy as np
from jax import lax
from jax.experimental import pallas as pl
from jax.experimental.pallas import tpu as pltpu
from jax.sharding import PartitionSpec as P

MAXE = 2
BLK = 32
VMEM_LIMIT = 56 * 1024 * 1024


def line_load(order):
    cuts = range(len(order) - 1)
    return max(sum(s > cut >= g for g, s in enumerate(order)) for cut in cuts)


@functools.lru_cache(None)
def routes(n):
    orders = list(itertools.permutations(range(n)))
    edges = [sum(1 << (g * n + s) for g, s in enumerate(order)) for order in orders]
    load = [line_load(order) for order in orders]
    codes = np.arange(1 << (n * n))
    table = np.zeros(codes.shape, np.int32)
    pairs = itertools.product(range(len(orders)), repeat=MAXE)
    for a, b in sorted(pairs, key=lambda p: -(load[p[0]] + load[p[1]])):
        word = a | b << 5
        for layer, i in enumerate((a, b)):
            for g, s in enumerate(orders[i]):
                word |= s << (10 + layer * 2 * n + 2 * g)
        table[codes & ~(edges[a] | edges[b]) == 0] = word
    return orders, table


def routed(index, n, back, value, work, operands):
    orders, _ = routes(n)

    def branch(order):
        pairs = [(s, g) if back else (g, s) for g, s in enumerate(order)]
        if all(s == g for s, g in pairs):
            return lambda v, *o: (v, work(*o))
        return lambda v, *o: (lax.ppermute(v, "group", pairs), work(*o))

    return lax.switch(index, [branch(order) for order in orders], value, *operands)


def pick_kernel(
    info_ref, slot_ref, count_ref, list_ref, tok_ref, dy_ref, prob_ref,
    first_ref, second_ref, pos_ref, expert_ref,
):
    experts, entries = list_ref.shape
    lanes = lax.broadcasted_iota(jnp.int32, (BLK, prob_ref.shape[1]), 1)
    for layer, out_ref in enumerate((first_ref, second_ref)):
        dest = info_ref[layer]
        expert = lax.fori_loop(
            0, experts, lambda e, found: jnp.where(slot_ref[e] == dest, e, found), 0
        )
        amount = jnp.where(dest >= 0, count_ref[info_ref[MAXE], expert], 0)
        expert_ref[layer] = expert

        @pl.loop(0, pos_ref.shape[1])
        def _(block):
            pos_ref[layer, block] = -1

        @pl.loop(0, entries)
        def _(j):
            target = pl.ds(pl.multiple_of(j * BLK, BLK), BLK)

            @pl.when(j < amount)
            def _():
                block = list_ref[expert, j]
                pos_ref[layer, block] = j
                source = pl.ds(pl.multiple_of(block * BLK, BLK), BLK)
                p = jnp.sum(
                    jnp.where(lanes == expert, prob_ref[source, :].astype(jnp.float32), 0.0),
                    axis=1,
                    keepdims=True,
                )
                out_ref[0, target, :] = tok_ref[source, :]
                out_ref[1, target, :] = (p * dy_ref[source, :].astype(jnp.float32)).astype(
                    out_ref.dtype
                )

            @pl.when(j >= amount)
            def _():
                nothing = jnp.zeros((BLK, out_ref.shape[2]), out_ref.dtype)
                out_ref[0, target, :] = nothing
                out_ref[1, target, :] = nothing


def put_kernel(pos_ref, expert_ref, prob_ref, first_ref, second_ref, out_ref, dx_ref):
    width = out_ref.shape[1]
    lanes = lax.broadcasted_iota(jnp.int32, (BLK, prob_ref.shape[1]), 1)

    @pl.loop(0, out_ref.shape[0] // BLK)
    def _(block):
        target = pl.ds(pl.multiple_of(block * BLK, BLK), BLK)
        probs = prob_ref[target, :].astype(jnp.float32)
        out = jnp.zeros((BLK, width), jnp.float32)
        dx = jnp.zeros((BLK, width), jnp.float32)
        for layer, home_ref in enumerate((first_ref, second_ref)):
            pos = pos_ref[layer, block]
            p = jnp.sum(jnp.where(lanes == expert_ref[layer], probs, 0.0), axis=1, keepdims=True)
            source = pl.ds(pl.multiple_of(jnp.maximum(pos, 0) * BLK, BLK), BLK)
            out += jnp.where(pos >= 0, home_ref[0, source, :].astype(jnp.float32), 0.0) * p
            dx += jnp.where(pos >= 0, home_ref[1, source, :].astype(jnp.float32), 0.0)
        out_ref[target, :] = out.astype(out_ref.dtype)
        dx_ref[target, :] = dx.astype(dx_ref.dtype)


MESH = pl.DeviceIdType.MESH
TILE = 16


def member_kernel(
    gate_ref, up_ref, back_ref, hid_ref, dg_ref, du_ref,
    recv0, recv1, recv2, send1, send2, kept, send_sem, recv_sem,
):
    ins, outs = (gate_ref, up_ref, back_ref), (hid_ref, dg_ref, du_ref)
    total, width = gate_ref.shape
    half, quarter, eighth, lanes = total // 2, total // 4, total // 8, width // 2
    f32 = jnp.float32
    m = lax.axis_index("member")
    core, x, y = m % 2, (m // 2) % 2, m // 4
    other, beside, across = m + 1 - 2 * core, m + 2 - 4 * x, m + 4 - 8 * y

    barrier = pltpu.get_barrier_semaphore()
    for partner in (other, beside, across):
        pl.semaphore_signal(barrier, inc=1, device_id={"member": partner}, device_id_type=MESH)
    pl.semaphore_wait(barrier, 3)

    first = ((x, beside), (y, across))
    second = ((y, across), (x, beside))
    columns = [pl.ds(h * lanes, lanes) for h in range(2)]
    copies = {}

    def rows(start, count):
        return pl.ds(pl.multiple_of(start, TILE), count)

    def send(step, h, k, source, target, to):
        copies[step, h, k] = pltpu.make_async_remote_copy(
            src_ref=source,
            dst_ref=target,
            send_sem=send_sem.at[step, h, k],
            recv_sem=recv_sem.at[step, h, k],
            device_id={"member": to},
            device_id_type=MESH,
        )
        copies[step, h, k].start()

    def arrived(step, h):
        for k in range(3):
            copies[step, h, k].wait_recv()

    for h in range(2):
        for k in range(3):
            source = ins[k].at[rows((1 - core) * half, half), columns[h]]
            send(0, h, k, source, recv0.at[h, k], other)
    for h in range(2):
        bit, to = first[h]
        arrived(0, h)

        def pair(start, k):
            mine = ins[k][rows(core * half + start, TILE), columns[h]].astype(f32)
            return mine + recv0[h, k, rows(start, TILE), :].astype(f32)

        @pl.loop(0, quarter // TILE)
        def _(t):
            for k in range(3):
                value = pair((1 - bit) * quarter + t * TILE, k)
                send1[h, k, rows(t * TILE, TILE), :] = value.astype(jnp.bfloat16)

        for k in range(3):
            send(1, h, k, send1.at[h, k], recv1.at[h, k], to)

        @pl.loop(0, quarter // TILE)
        def _(t):
            for k in range(3):
                kept[h, k, rows(t * TILE, TILE), :] = pair(bit * quarter + t * TILE, k)

    for h in range(2):
        bit, to = second[h]
        arrived(1, h)

        @pl.loop(0, eighth // TILE)
        def _(t):
            for k in range(3):
                at = rows((1 - bit) * eighth + t * TILE, TILE)
                value = kept[h, k, at, :] + recv1[h, k, at, :].astype(f32)
                send2[h, k, rows(t * TILE, TILE), :] = value.astype(jnp.bfloat16)

        for k in range(3):
            send(2, h, k, send2.at[h, k], recv2.at[h, k], to)

    for h in range(2):
        bit, to = second[h]
        arrived(2, h)
        home = core * half + first[h][0] * quarter + bit * eighth

        @pl.loop(0, eighth // TILE)
        def _(t):
            at = rows(bit * eighth + t * TILE, TILE)
            gate, up, back = (
                kept[h, k, at, :]
                + recv1[h, k, at, :].astype(f32)
                + recv2[h, k, rows(t * TILE, TILE), :].astype(f32)
                for k in range(3)
            )
            there = rows(home + t * TILE, TILE)
            for ref, value in zip(outs, activations(gate, up, back)):
                ref[there, columns[h]] = value

        for k in range(3):
            block = outs[k].at[rows(home, eighth), columns[h]]
            send(3, h, k, block, block, to)
    for h in range(2):
        bit, to = first[h]
        arrived(3, h)
        for k in range(3):
            block = outs[k].at[rows(core * half + bit * quarter, quarter), columns[h]]
            send(4, h, k, block, block, to)
    for h in range(2):
        arrived(4, h)
        for k in range(3):
            block = outs[k].at[rows(core * half, half), columns[h]]
            send(5, h, k, block, block, other)
    for h in range(2):
        arrived(5, h)
    for copy in copies.values():
        copy.wait_send()


def member_call(gate, up, back):
    total, width = gate.shape
    lanes = width // 2
    bf16 = jnp.bfloat16
    return pl.pallas_call(
        member_kernel,
        out_shape=[jax.ShapeDtypeStruct(gate.shape, bf16)] * 3,
        in_specs=[VMEM] * 3,
        out_specs=[VMEM] * 3,
        scratch_shapes=[
            pltpu.VMEM((2, 3, total // 2, lanes), bf16),
            pltpu.VMEM((2, 3, total // 4, lanes), bf16),
            pltpu.VMEM((2, 3, total // 8, lanes), bf16),
            pltpu.VMEM((2, 3, total // 4, lanes), bf16),
            pltpu.VMEM((2, 3, total // 8, lanes), bf16),
            pltpu.VMEM((2, 3, total // 4, lanes), jnp.float32),
            pltpu.SemaphoreType.DMA((6, 2, 3)),
            pltpu.SemaphoreType.DMA((6, 2, 3)),
        ],
        compiler_params=pltpu.CompilerParams(
            collective_id=0, has_side_effects=True, vmem_limit_bytes=VMEM_LIMIT
        ),
    )(gate, up, back)


def activations(gate, up, back):
    s = jax.nn.sigmoid(gate)
    return (
        (gate * s * up).astype(jnp.bfloat16),
        (back * up * s * (1.0 + gate * (1.0 - s))).astype(jnp.bfloat16),
        (back * gate * s).astype(jnp.bfloat16),
    )


SMEM = pl.BlockSpec(memory_space=pltpu.SMEM)
VMEM = pl.BlockSpec(memory_space=pltpu.VMEM)


def body(
    tokens, grad_output, gate_prob, w_gate, w_up, w_down, expert_slot, block_counts, block_lists
):
    width = tokens.shape[1]
    n = lax.axis_size("group")
    members = lax.axis_size("member")
    block_total = tokens.shape[0] // BLK
    layer_rows = block_lists.shape[2] * BLK
    me = lax.axis_index("group")
    wg, wu, wd = w_gate[0], w_up[0], w_down[0]
    f32 = jnp.float32

    slot_ids = jnp.arange(n, dtype=jnp.int32)
    at_slot = expert_slot[:, None] == slot_ids[None, :]
    used = jnp.any((block_counts > 0)[:, :, None] & at_slot[None, :, :], axis=1)
    layers = jnp.arange(MAXE, dtype=jnp.int32)
    small = n == 4
    if small:
        bits = (1 << np.arange(n * n)).reshape(n, n).astype(np.int32)
        word = jnp.asarray(routes(n)[1])[jnp.sum(used * bits)]
        index = (word & 31, word >> 5 & 31)
        dests = word >> (10 + 2 * n * layers + 2 * me) & 3
        my_dest = jnp.where((layers > 0) & (dests == dests[0]), -1, dests)
    else:
        mine = lax.dynamic_index_in_dim(used, me, 0, keepdims=False)
        rank = jnp.cumsum(mine.astype(jnp.int32)) - 1
        hit = mine[None, :] & (rank[None, :] == layers[:, None])
        my_dest = jnp.sum(hit * (slot_ids + 1)[None, :], axis=1) - 1
    info = jnp.concatenate([my_dest.astype(jnp.int32), me[None].astype(jnp.int32)])

    rows_shape = jax.ShapeDtypeStruct((2, layer_rows, width), jnp.bfloat16)
    sent_a, sent_b, position, my_expert = pl.pallas_call(
        pick_kernel,
        out_shape=[
            rows_shape,
            rows_shape,
            jax.ShapeDtypeStruct((MAXE, block_total), jnp.int32),
            jax.ShapeDtypeStruct((MAXE,), jnp.int32),
        ],
        in_specs=[SMEM] * 4 + [VMEM] * 3,
        out_specs=[VMEM, VMEM, SMEM, SMEM],
        compiler_params=pltpu.CompilerParams(vmem_limit_bytes=VMEM_LIMIT),
    )(info, expert_slot, block_counts, block_lists[0], tokens, grad_output, gate_prob)

    def dot(a, b, dims):
        return lax.dot_general(a, b, (dims, ((), ())), preferred_element_type=f32).astype(
            jnp.bfloat16
        )

    def enter(rows, wg, wu, wd):
        return (
            dot(rows[0], wg, ((1,), (0,))),
            dot(rows[0], wu, ((1,), (0,))),
            dot(rows[1], wd, ((1,), (1,))),
        )

    def leave(hidden, d_gate, d_up, wg, wu, wd):
        dx = lax.dot_general(
            d_gate, wg, (((1,), (1,)), ((), ())), preferred_element_type=f32
        ) + lax.dot_general(d_up, wu, (((1,), (1,)), ((), ())), preferred_element_type=f32)
        return jnp.stack([dot(hidden, wd, ((1,), (0,))), dx.astype(jnp.bfloat16)])

    def panel(rows, grads):
        return dot(rows, grads, ((0,), (0,)))

    if small:
        got_a, _ = routed(index[0], n, False, sent_a, lambda: (), ())
        got_b, parts_a = routed(index[1], n, False, sent_b, enter, (got_a, wg, wu, wd))
    else:
        place = (my_dest[:, None] == slot_ids[None, :]).astype(jnp.bfloat16)
        spread = jnp.einsum("ln,lkrw->nkrw", place, jnp.stack([sent_a, sent_b]))
        came = lax.all_to_all(spread, "group", split_axis=0, concat_axis=0, tiled=True)
        users = lax.dynamic_index_in_dim(used, me, 1, keepdims=False).astype(jnp.int32)
        user_rank = jnp.cumsum(users) - 1
        take = ((user_rank[None, :] == layers[:, None]) & (users[None, :] > 0)).astype(jnp.bfloat16)
        got_a, got_b = jnp.einsum("ln,nkrw->lkrw", take, came)
        parts_a = enter(got_a, wg, wu, wd)
    parts = [
        jnp.concatenate(pair, axis=0) for pair in zip(parts_a, enter(got_b, wg, wu, wd))
    ]
    if members == 8 and 2 * layer_rows % (8 * TILE) == 0:
        acts = member_call(*parts)
    else:
        summed = lax.psum_scatter(
            jnp.concatenate(parts, axis=1), "member", scatter_dimension=0, tiled=True
        )
        acts = jnp.concatenate(activations(*jnp.split(summed.astype(f32), 3, axis=1)), axis=1)
        acts = lax.all_gather(acts, "member", axis=0, tiled=True)
        acts = jnp.split(acts, 3, axis=1)
    hidden, d_gate, d_up = acts
    rows_x = jnp.concatenate([got_a[0], got_b[0]], axis=0)
    rows_dy = jnp.concatenate([got_a[1], got_b[1]], axis=0)
    both_a = leave(*(act[:layer_rows] for act in acts), wg, wu, wd)
    acts_b = tuple(act[layer_rows:] for act in acts)
    if small:

        def beside_a(rows_x, d_gate, acts_b, wg, wu, wd):
            return leave(*acts_b, wg, wu, wd), panel(rows_x, d_gate)

        def beside_b(rows_x, rows_dy, hidden, d_up):
            return panel(rows_x, d_up), panel(hidden, rows_dy)

        home_a, (both_b, grad_gate) = routed(
            index[0], n, True, both_a, beside_a, (rows_x, d_gate, acts_b, wg, wu, wd)
        )
        home_b, (grad_up, grad_down) = routed(
            index[1], n, True, both_b, beside_b, (rows_x, rows_dy, hidden, d_up)
        )
    else:
        both_b = leave(*acts_b, wg, wu, wd)
        spread = jnp.einsum("ln,lkrw->nkrw", take, jnp.stack([both_a, both_b]))
        came = lax.all_to_all(spread, "group", split_axis=0, concat_axis=0, tiled=True)
        home_a, home_b = jnp.einsum("ln,nkrw->lkrw", place, came)
        grad_gate, grad_up = panel(rows_x, d_gate), panel(rows_x, d_up)
        grad_down = panel(hidden, rows_dy)
    layer_output, grad_input = pl.pallas_call(
        put_kernel,
        out_shape=[jax.ShapeDtypeStruct(tokens.shape, jnp.bfloat16)] * 2,
        in_specs=[SMEM, SMEM, VMEM, VMEM, VMEM],
        out_specs=[VMEM, VMEM],
        compiler_params=pltpu.CompilerParams(vmem_limit_bytes=VMEM_LIMIT),
    )(position, my_expert, gate_prob, home_a, home_b)
    return (layer_output, grad_input, grad_gate[None], grad_up[None], grad_down[None])


def solution(mesh):
    in_specs = (
        P("group", "member"),
        P("group", "member"),
        P("group", None),
        P("group", "member", None),
        P("group", "member", None),
        P("group", None, "member"),
        P(),
        P(),
        P("group", None, None),
    )
    out_specs = (
        P("group", "member"),
        P("group", "member"),
        P("group", "member", None),
        P("group", "member", None),
        P("group", None, "member"),
    )
    return jax.shard_map(body, mesh=mesh, in_specs=in_specs, out_specs=out_specs, check_vma=False)
```

```python
import functools
import itertools

import jax
import jax.numpy as jnp
import numpy as np
from jax import lax
from jax.experimental import pallas as pl
from jax.experimental.pallas import tpu as pltpu
from jax.sharding import PartitionSpec as P

MAXE = 2
BLK = 32
VMEM_LIMIT = 56 * 1024 * 1024


def line_load(order):
    cuts = range(len(order) - 1)
    return max(sum(s > cut >= g for g, s in enumerate(order)) for cut in cuts)


@functools.lru_cache(None)
def routes(n):
    orders = list(itertools.permutations(range(n)))
    edges = [sum(1 << (g * n + s) for g, s in enumerate(order)) for order in orders]
    load = [line_load(order) for order in orders]
    codes = np.arange(1 << (n * n))
    table = np.zeros(codes.shape, np.int32)
    pairs = itertools.product(range(len(orders)), repeat=MAXE)
    for a, b in sorted(pairs, key=lambda p: -(load[p[0]] + load[p[1]])):
        word = a | b << 5
        for layer, i in enumerate((a, b)):
            for g, s in enumerate(orders[i]):
                word |= s << (10 + layer * 2 * n + 2 * g)
        table[codes & ~(edges[a] | edges[b]) == 0] = word
    return orders, table


def routed(index, n, back, value):
    orders, _ = routes(n)

    def branch(order):
        pairs = [(s, g) if back else (g, s) for g, s in enumerate(order)]
        if all(s == g for s, g in pairs):
            return lambda v: v
        return lambda v: lax.ppermute(v, "group", pairs)

    return lax.switch(index, [branch(order) for order in orders], value)


def pick_kernel(
    info_ref, slot_ref, count_ref, list_ref, tok_ref, dy_ref, prob_ref,
    first_ref, second_ref, pos_ref, expert_ref,
):
    experts, entries = list_ref.shape
    lanes = lax.broadcasted_iota(jnp.int32, (BLK, prob_ref.shape[1]), 1)
    for layer, out_ref in enumerate((first_ref, second_ref)):
        dest = info_ref[layer]
        expert = lax.fori_loop(
            0, experts, lambda e, found: jnp.where(slot_ref[e] == dest, e, found), 0
        )
        amount = jnp.where(dest >= 0, count_ref[info_ref[MAXE], expert], 0)
        expert_ref[layer] = expert

        @pl.loop(0, pos_ref.shape[1])
        def _(block):
            pos_ref[layer, block] = -1

        @pl.loop(0, entries)
        def _(j):
            target = pl.ds(pl.multiple_of(j * BLK, BLK), BLK)

            @pl.when(j < amount)
            def _():
                block = list_ref[expert, j]
                pos_ref[layer, block] = j
                source = pl.ds(pl.multiple_of(block * BLK, BLK), BLK)
                p = jnp.sum(
                    jnp.where(lanes == expert, prob_ref[source, :].astype(jnp.float32), 0.0),
                    axis=1,
                    keepdims=True,
                )
                out_ref[0, target, :] = tok_ref[source, :]
                out_ref[1, target, :] = (p * dy_ref[source, :].astype(jnp.float32)).astype(
                    out_ref.dtype
                )

            @pl.when(j >= amount)
            def _():
                nothing = jnp.zeros((BLK, out_ref.shape[2]), out_ref.dtype)
                out_ref[0, target, :] = nothing
                out_ref[1, target, :] = nothing


def put_kernel(pos_ref, expert_ref, prob_ref, first_ref, second_ref, out_ref, dx_ref):
    width = out_ref.shape[1]
    lanes = lax.broadcasted_iota(jnp.int32, (BLK, prob_ref.shape[1]), 1)

    @pl.loop(0, out_ref.shape[0] // BLK)
    def _(block):
        target = pl.ds(pl.multiple_of(block * BLK, BLK), BLK)
        probs = prob_ref[target, :].astype(jnp.float32)
        out = jnp.zeros((BLK, width), jnp.float32)
        dx = jnp.zeros((BLK, width), jnp.float32)
        for layer, home_ref in enumerate((first_ref, second_ref)):
            pos = pos_ref[layer, block]
            p = jnp.sum(jnp.where(lanes == expert_ref[layer], probs, 0.0), axis=1, keepdims=True)
            source = pl.ds(pl.multiple_of(jnp.maximum(pos, 0) * BLK, BLK), BLK)
            out += jnp.where(pos >= 0, home_ref[0, source, :].astype(jnp.float32), 0.0) * p
            dx += jnp.where(pos >= 0, home_ref[1, source, :].astype(jnp.float32), 0.0)
        out_ref[target, :] = out.astype(out_ref.dtype)
        dx_ref[target, :] = dx.astype(dx_ref.dtype)


MESH = pl.DeviceIdType.MESH
TILE = 16
CHUNKS = 4


def member_kernel(
    gate_ref, up_ref, back_ref, hid_ref, dg_ref, du_ref,
    recv0, recv1, recv2, send1, send2, kept, send_sem, recv_sem,
):
    ins, outs = (gate_ref, up_ref, back_ref), (hid_ref, dg_ref, du_ref)
    total, width = gate_ref.shape
    half, quarter, eighth, lanes = total // 2, total // 4, total // 8, width // CHUNKS
    f32 = jnp.float32
    m = lax.axis_index("member")
    core, x, y = m % 2, (m // 2) % 2, m // 4
    other, beside, across = m + 1 - 2 * core, m + 2 - 4 * x, m + 4 - 8 * y

    barrier = pltpu.get_barrier_semaphore()
    for partner in (other, beside, across):
        pl.semaphore_signal(barrier, inc=1, device_id={"member": partner}, device_id_type=MESH)
    pl.semaphore_wait(barrier, 3)

    first = ((x, beside), (y, across)) * (CHUNKS // 2)
    second = ((y, across), (x, beside)) * (CHUNKS // 2)
    columns = [pl.ds(h * lanes, lanes) for h in range(CHUNKS)]
    copies = {}

    def rows(start, count):
        return pl.ds(pl.multiple_of(start, TILE), count)

    def send(step, h, k, source, target, to):
        copies[step, h, k] = pltpu.make_async_remote_copy(
            src_ref=source,
            dst_ref=target,
            send_sem=send_sem.at[step, h, k],
            recv_sem=recv_sem.at[step, h, k],
            device_id={"member": to},
            device_id_type=MESH,
        )
        copies[step, h, k].start()

    def arrived(step, h):
        for k in range(3):
            copies[step, h, k].wait_recv()

    for h in range(CHUNKS):
        for k in range(3):
            source = ins[k].at[rows((1 - core) * half, half), columns[h]]
            send(0, h, k, source, recv0.at[h, k], other)
    for h in range(CHUNKS):
        bit, to = first[h]
        arrived(0, h)

        def pair(start, k):
            mine = ins[k][rows(core * half + start, TILE), columns[h]].astype(f32)
            return mine + recv0[h, k, rows(start, TILE), :].astype(f32)

        @pl.loop(0, quarter // TILE)
        def _(t):
            for k in range(3):
                value = pair((1 - bit) * quarter + t * TILE, k)
                send1[h, k, rows(t * TILE, TILE), :] = value.astype(jnp.bfloat16)

        for k in range(3):
            send(1, h, k, send1.at[h, k], recv1.at[h, k], to)

        @pl.loop(0, quarter // TILE)
        def _(t):
            for k in range(3):
                kept[h, k, rows(t * TILE, TILE), :] = pair(bit * quarter + t * TILE, k)

    for h in range(CHUNKS):
        bit, to = second[h]
        arrived(1, h)

        @pl.loop(0, eighth // TILE)
        def _(t):
            for k in range(3):
                at = rows((1 - bit) * eighth + t * TILE, TILE)
                value = kept[h, k, at, :] + recv1[h, k, at, :].astype(f32)
                send2[h, k, rows(t * TILE, TILE), :] = value.astype(jnp.bfloat16)

        for k in range(3):
            send(2, h, k, send2.at[h, k], recv2.at[h, k], to)

    for h in range(CHUNKS):
        bit, to = second[h]
        arrived(2, h)
        home = core * half + first[h][0] * quarter + bit * eighth

        @pl.loop(0, eighth // TILE)
        def _(t):
            at = rows(bit * eighth + t * TILE, TILE)
            gate, up, back = (
                kept[h, k, at, :]
                + recv1[h, k, at, :].astype(f32)
                + recv2[h, k, rows(t * TILE, TILE), :].astype(f32)
                for k in range(3)
            )
            there = rows(home + t * TILE, TILE)
            for ref, value in zip(outs, activations(gate, up, back)):
                ref[there, columns[h]] = value

        for k in range(3):
            block = outs[k].at[rows(home, eighth), columns[h]]
            send(3, h, k, block, block, to)
    for h in range(CHUNKS):
        bit, to = first[h]
        arrived(3, h)
        for k in range(3):
            block = outs[k].at[rows(core * half + bit * quarter, quarter), columns[h]]
            send(4, h, k, block, block, to)
    for h in range(CHUNKS):
        arrived(4, h)
        for k in range(3):
            block = outs[k].at[rows(core * half, half), columns[h]]
            send(5, h, k, block, block, other)
    for h in range(CHUNKS):
        arrived(5, h)
    for copy in copies.values():
        copy.wait_send()


def member_call(gate, up, back):
    total, width = gate.shape
    lanes = width // CHUNKS
    bf16 = jnp.bfloat16
    return pl.pallas_call(
        member_kernel,
        out_shape=[jax.ShapeDtypeStruct(gate.shape, bf16)] * 3,
        in_specs=[VMEM] * 3,
        out_specs=[VMEM] * 3,
        scratch_shapes=[
            pltpu.VMEM((CHUNKS, 3, total // 2, lanes), bf16),
            pltpu.VMEM((CHUNKS, 3, total // 4, lanes), bf16),
            pltpu.VMEM((CHUNKS, 3, total // 8, lanes), bf16),
            pltpu.VMEM((CHUNKS, 3, total // 4, lanes), bf16),
            pltpu.VMEM((CHUNKS, 3, total // 8, lanes), bf16),
            pltpu.VMEM((CHUNKS, 3, total // 4, lanes), jnp.float32),
            pltpu.SemaphoreType.DMA((6, CHUNKS, 3)),
            pltpu.SemaphoreType.DMA((6, CHUNKS, 3)),
        ],
        compiler_params=pltpu.CompilerParams(
            collective_id=0, has_side_effects=True, vmem_limit_bytes=VMEM_LIMIT
        ),
    )(gate, up, back)


def activations(gate, up, back):
    s = jax.nn.sigmoid(gate)
    return (
        (gate * s * up).astype(jnp.bfloat16),
        (back * up * s * (1.0 + gate * (1.0 - s))).astype(jnp.bfloat16),
        (back * gate * s).astype(jnp.bfloat16),
    )


SMEM = pl.BlockSpec(memory_space=pltpu.SMEM)
VMEM = pl.BlockSpec(memory_space=pltpu.VMEM)


def body(
    tokens, grad_output, gate_prob, w_gate, w_up, w_down, expert_slot, block_counts, block_lists
):
    width = tokens.shape[1]
    n = lax.axis_size("group")
    members = lax.axis_size("member")
    block_total = tokens.shape[0] // BLK
    layer_rows = block_lists.shape[2] * BLK
    me = lax.axis_index("group")
    wg, wu, wd = w_gate[0], w_up[0], w_down[0]
    f32 = jnp.float32

    slot_ids = jnp.arange(n, dtype=jnp.int32)
    at_slot = expert_slot[:, None] == slot_ids[None, :]
    used = jnp.any((block_counts > 0)[:, :, None] & at_slot[None, :, :], axis=1)
    layers = jnp.arange(MAXE, dtype=jnp.int32)
    small = n == 4
    if small:
        bits = (1 << np.arange(n * n)).reshape(n, n).astype(np.int32)
        word = jnp.asarray(routes(n)[1])[jnp.sum(used * bits)]
        index = (word & 31, word >> 5 & 31)
        dests = word >> (10 + 2 * n * layers + 2 * me) & 3
        my_dest = jnp.where((layers > 0) & (dests == dests[0]), -1, dests)
    else:
        mine = lax.dynamic_index_in_dim(used, me, 0, keepdims=False)
        rank = jnp.cumsum(mine.astype(jnp.int32)) - 1
        hit = mine[None, :] & (rank[None, :] == layers[:, None])
        my_dest = jnp.sum(hit * (slot_ids + 1)[None, :], axis=1) - 1
    info = jnp.concatenate([my_dest.astype(jnp.int32), me[None].astype(jnp.int32)])

    rows_shape = jax.ShapeDtypeStruct((2, layer_rows, width), jnp.bfloat16)
    sent_a, sent_b, position, my_expert = pl.pallas_call(
        pick_kernel,
        out_shape=[
            rows_shape,
            rows_shape,
            jax.ShapeDtypeStruct((MAXE, block_total), jnp.int32),
            jax.ShapeDtypeStruct((MAXE,), jnp.int32),
        ],
        in_specs=[SMEM] * 4 + [VMEM] * 3,
        out_specs=[VMEM, VMEM, SMEM, SMEM],
        compiler_params=pltpu.CompilerParams(vmem_limit_bytes=VMEM_LIMIT),
    )(info, expert_slot, block_counts, block_lists[0], tokens, grad_output, gate_prob)

    def dot(a, b, dims):
        return lax.dot_general(a, b, (dims, ((), ())), preferred_element_type=f32).astype(
            jnp.bfloat16
        )

    def leave(hidden, d_gate, d_up, wg, wu, wd):
        dx = lax.dot_general(
            d_gate, wg, (((1,), (1,)), ((), ())), preferred_element_type=f32
        ) + lax.dot_general(d_up, wu, (((1,), (1,)), ((), ())), preferred_element_type=f32)
        return jnp.stack([dot(hidden, wd, ((1,), (0,))), dx.astype(jnp.bfloat16)])

    def panel(rows, grads):
        return dot(rows, grads, ((0,), (0,)))

    if small:
        got_a = routed(index[0], n, False, sent_a)
        got_b = routed(index[1], n, False, sent_b)
    else:
        place = (my_dest[:, None] == slot_ids[None, :]).astype(jnp.bfloat16)
        spread = jnp.einsum("ln,lkrw->nkrw", place, jnp.stack([sent_a, sent_b]))
        came = lax.all_to_all(spread, "group", split_axis=0, concat_axis=0, tiled=True)
        users = lax.dynamic_index_in_dim(used, me, 1, keepdims=False).astype(jnp.int32)
        user_rank = jnp.cumsum(users) - 1
        take = ((user_rank[None, :] == layers[:, None]) & (users[None, :] > 0)).astype(jnp.bfloat16)
        got_a, got_b = jnp.einsum("ln,nkrw->lkrw", take, came)
    rows_x = jnp.concatenate([got_a[0], got_b[0]], axis=0)
    rows_dy = jnp.concatenate([got_a[1], got_b[1]], axis=0)
    parts = [
        dot(rows_x, wg, ((1,), (0,))),
        dot(rows_x, wu, ((1,), (0,))),
        dot(rows_dy, wd, ((1,), (1,))),
    ]
    if members == 8 and 2 * layer_rows % (8 * TILE) == 0:
        acts = member_call(*parts)
    else:
        summed = lax.psum_scatter(
            jnp.concatenate(parts, axis=1), "member", scatter_dimension=0, tiled=True
        )
        acts = jnp.concatenate(activations(*jnp.split(summed.astype(f32), 3, axis=1)), axis=1)
        acts = lax.all_gather(acts, "member", axis=0, tiled=True)
        acts = jnp.split(acts, 3, axis=1)
    hidden, d_gate, d_up = acts
    both_a = leave(*(act[:layer_rows] for act in acts), wg, wu, wd)
    both_b = leave(*(act[layer_rows:] for act in acts), wg, wu, wd)
    if small:
        home_a = routed(index[0], n, True, both_a)
        home_b = routed(index[1], n, True, both_b)
    else:
        spread = jnp.einsum("ln,lkrw->nkrw", take, jnp.stack([both_a, both_b]))
        came = lax.all_to_all(spread, "group", split_axis=0, concat_axis=0, tiled=True)
        home_a, home_b = jnp.einsum("ln,nkrw->lkrw", place, came)
    grad_gate, grad_up = panel(rows_x, d_gate), panel(rows_x, d_up)
    grad_down = panel(hidden, rows_dy)
    layer_output, grad_input = pl.pallas_call(
        put_kernel,
        out_shape=[jax.ShapeDtypeStruct(tokens.shape, jnp.bfloat16)] * 2,
        in_specs=[SMEM, SMEM, VMEM, VMEM, VMEM],
        out_specs=[VMEM, VMEM],
        compiler_params=pltpu.CompilerParams(vmem_limit_bytes=VMEM_LIMIT),
    )(position, my_expert, gate_prob, home_a, home_b)
    return (layer_output, grad_input, grad_gate[None], grad_up[None], grad_down[None])


def solution(mesh):
    in_specs = (
        P("group", "member"),
        P("group", "member"),
        P("group", None),
        P("group", "member", None),
        P("group", "member", None),
        P("group", None, "member"),
        P(),
        P(),
        P("group", None, None),
    )
    out_specs = (
        P("group", "member"),
        P("group", "member"),
        P("group", "member", None),
        P("group", "member", None),
        P("group", None, "member"),
    )
    return jax.shard_map(body, mesh=mesh, in_specs=in_specs, out_specs=out_specs, check_vma=False)
```
